128 devices in a mesh: dp: 16 (over z_lo, x, core), mp: 8 (over y, z_hi).
Axes of the slice: x: 4, y: 4, z: 4 (z_hi: 2, z_lo: 2; z = z_hi * 2 + z_lo), core: 2. Of those that a mesh axis runs over, the one named last changes fastest.
Arguments:
- tokens: bfloat16 [1024, 18432], P('mp', 'dp'), may hold values from -6 to 6
- gate_weight: bfloat16 [18432, 8192], P('dp', 'mp'), may hold values from -0.046875 to 0.046875
- up_weight: bfloat16 [18432, 8192], P('dp', 'mp'), may hold values from -0.046875 to 0.046875
- down_weight: bfloat16 [8192, 18432], P('mp', 'dp'), may hold values from -0.0625 to 0.0625
- cotangent: bfloat16 [1024, 18432], P('mp', 'dp'), may hold values from -1.5 to 1.5
Outputs:
- mixed: bfloat16 [1024, 18432], P('mp', 'dp')
- grad_tokens: bfloat16 [1024, 18432], P('mp', 'dp')
- grad_gate: float32 [18432, 8192], P('dp', 'mp')
- grad_up: float32 [18432, 8192], P('dp', 'mp')
- grad_down: float32 [8192, 18432], P('mp', 'dp')
The draws below stay inside these ranges and needn't reach their ends.
All inputs are finite; a program needn't handle non-finite values.
Results may differ from the reference program's by a relative error of at most 0.0049.
Values may be sent and summed in bfloat16 or wider, within the bound.
A program may use at most 128 MiB of HBM per device.

```python
import jax
import jax.numpy as jnp

D = 18432
TOKENS = 1024
FF = 8192


def block_scale(own_key, dims, pieces, low, largest):
    def one(position, shards_of):
        draws = jax.random.uniform(jax.random.fold_in(jax.random.fold_in(own_key, 6), position), (shards_of,), jnp.float32, low / len(pieces), largest / len(pieces))
        return jnp.repeat(jnp.exp(draws), dims[position] // shards_of).reshape((-1,) + (1,) * (len(dims) - position - 1))

    gain = one(*pieces[0])
    for cut in pieces[1:]:
        gain = gain * one(*cut)
    return gain


def centred(own_key, extent, deviation, reach, shards=(), held_as=jnp.bfloat16):
    loudness = block_scale(own_key, extent, shards, -0.22, 0.18) if shards else 1.0
    array = jax.random.normal(own_key, extent, jnp.float32) * deviation * loudness
    return jnp.minimum(jnp.maximum(array, -reach), reach).astype(held_as)


def setup_inputs(seed: int = 0) -> dict:
    splits = jax.random.split(jax.random.key(seed), 6)
    tokens = centred(splits[0], (TOKENS, D), 1.0, 6.0, ((0, 8), (1, 16)))
    gate_weight = centred(splits[1], (D, FF), D ** -0.5, 0.046875, ((0, 16), (1, 8)))
    up_weight = centred(splits[2], (D, FF), D ** -0.5, 0.046875, ((0, 16), (1, 8)))
    down_weight = centred(splits[3], (FF, D), FF ** -0.5, 0.0625, ((0, 8), (1, 16)))
    cotangent = centred(splits[4], (TOKENS, D), 0.25, 1.5, ((0, 8), (1, 16)))
    return dict(tokens=tokens, gate_weight=gate_weight, up_weight=up_weight, down_weight=down_weight, cotangent=cotangent)


def reference(tokens, gate_weight, up_weight, down_weight, cotangent):
    gate = jnp.dot(tokens, gate_weight, preferred_element_type=jnp.float32)
    up = jnp.dot(tokens, up_weight, preferred_element_type=jnp.float32)
    sigma = jax.nn.sigmoid(gate)
    hidden = (gate * sigma * up).astype(jnp.bfloat16)
    mixed = jnp.dot(hidden, down_weight, preferred_element_type=jnp.float32).astype(jnp.bfloat16)
    grad_hidden = jnp.dot(cotangent, down_weight.T, preferred_element_type=jnp.float32)
    grad_gate_pre = (grad_hidden * up * sigma * (1.0 + gate * (1.0 - sigma))).astype(jnp.bfloat16)
    grad_up_pre = (grad_hidden * gate * sigma).astype(jnp.bfloat16)
    grad_tokens = (jnp.dot(grad_gate_pre, gate_weight.T, preferred_element_type=jnp.float32)
                   + jnp.dot(grad_up_pre, up_weight.T, preferred_element_type=jnp.float32)).astype(jnp.bfloat16)
    grad_gate = jnp.dot(tokens.T, grad_gate_pre, preferred_element_type=jnp.float32)
    grad_up = jnp.dot(tokens.T, grad_up_pre, preferred_element_type=jnp.float32)
    grad_down = jnp.dot(hidden.T, cotangent, preferred_element_type=jnp.float32)
    return mixed, grad_tokens, grad_gate, grad_up, grad_down
```

```python
import jax
import jax.numpy as jnp
from jax import lax
from jax.sharding import PartitionSpec as P


def times_transposed(left, right):
    return lax.dot_general(
        left, right, (((1,), (1,)), ((), ())), preferred_element_type=jnp.float32
    )


def inner_rows(left, right):
    return lax.dot_general(
        left, right, (((0,), (0,)), ((), ())), preferred_element_type=jnp.float32
    )


def scatter_sum(part, axis):
    return lax.psum_scatter(part, axis, scatter_dimension=0, tiled=True)


def gather(part, axis):
    return lax.all_gather(part, axis, axis=0, tiled=True)


def on_device(tokens, gate_weight, up_weight, down_weight, cotangent):
    rows_all = gather(tokens, "mp")
    cot_all = gather(cotangent, "mp")
    gate = scatter_sum(jnp.dot(rows_all, gate_weight, preferred_element_type=jnp.float32), "dp")
    up = scatter_sum(jnp.dot(rows_all, up_weight, preferred_element_type=jnp.float32), "dp")
    grad_hidden = scatter_sum(times_transposed(cot_all, down_weight), "dp")
    sigma = jax.nn.sigmoid(gate)
    hidden = (gate * sigma * up).astype(jnp.bfloat16)
    hidden = gather(hidden, "dp")
    mixed = scatter_sum(jnp.dot(hidden, down_weight, preferred_element_type=jnp.float32), "mp").astype(jnp.bfloat16)
    grad_gate_pre = (grad_hidden * up * sigma * (1.0 + gate * (1.0 - sigma))).astype(jnp.bfloat16)
    grad_up_pre = (grad_hidden * gate * sigma).astype(jnp.bfloat16)
    grad_gate_pre = gather(grad_gate_pre, "dp")
    grad_up_pre = gather(grad_up_pre, "dp")
    grad_tokens = scatter_sum(
        times_transposed(grad_gate_pre, gate_weight) + times_transposed(grad_up_pre, up_weight),
        "mp",
    ).astype(jnp.bfloat16)
    grad_gate = inner_rows(rows_all, grad_gate_pre)
    grad_up = inner_rows(rows_all, grad_up_pre)
    grad_down = inner_rows(hidden, cot_all)
    return (mixed, grad_tokens, grad_gate, grad_up, grad_down)


def solution(mesh):
    in_specs = (P("mp", "dp"), P("dp", "mp"), P("dp", "mp"), P("mp", "dp"), P("mp", "dp"))
    out_specs = (P("mp", "dp"), P("mp", "dp"), P("dp", "mp"), P("dp", "mp"), P("mp", "dp"))
    return jax.shard_map(
        on_device, mesh=mesh, in_specs=in_specs, out_specs=out_specs, check_vma=False
    )
```

```python
import functools

import jax
import jax.numpy as jnp
from jax import lax
from jax.experimental import pallas as pl
from jax.experimental.pallas import tpu as pltpu
from jax.sharding import PartitionSpec as P

MESH = pl.DeviceIdType.MESH
F32 = jnp.float32
BF16 = jnp.bfloat16
CHUNKS = 4
Y, X = 4, 4


def dot(left, right):
    return lax.dot_general(left, right, (((1,), (0,)), ((), ())), preferred_element_type=F32)


def dot_t(left, right):
    return lax.dot_general(left, right, (((1,), (1,)), ((), ())), preferred_element_type=F32)


def inner_rows(left, right):
    return lax.dot_general(left, right, (((0,), (0,)), ((), ())), preferred_element_type=F32)


COLUMNS = {}
for name, copies in (
    ("tok_z", 1), ("cot_y", 3), ("tok_y", 3), ("cot_z", 1),
    ("core0", 1), ("core1", 1), ("x0", 3), ("x1", 3), ("z0", 1), ("z1", 1),
    ("back_z0", 1), ("back_z1", 1), ("back_x0", 3), ("back_x1", 3), ("back_c0", 1), ("back_c1", 1),
    ("mix_y", 3), ("mix_z", 1), ("gt_z", 1), ("gt_y", 3),
):
    COLUMNS[name] = (sum(n for _, n in COLUMNS.values()), copies)
TOTAL = sum(n for _, n in COLUMNS.values())


def kernel(
    tokens, gate_w, up_w, down_w, cotangent,
    mixed, grad_tokens, tok_out, cot_out, hid_out, ggp_out, gup_out,
    gw, uw, dw, tok, cot, part, crecv, xs, xr, xown, zr, full, tmp,
    ms, mown, mr, mz, mzr, gs, gown, gr, gys, gyr,
    send_sem, recv_sem, load_sem, own_sem, out_sem,
):
    rows = 128 // CHUNKS
    height = 1024 // CHUNKS
    share = height // 16
    dp, mp = lax.axis_index("dp"), lax.axis_index("mp")
    core = lax.rem(dp, 2)
    x = lax.rem(dp // 2, 4)
    zl = dp // 8
    y = mp // 2
    zh = lax.rem(mp, 2)

    def at_x(k):
        return (zl * 8 + lax.rem(x + k, 4) * 2 + core, mp)

    def at_y(k):
        return (dp, lax.rem(y + k, 4) * 2 + zh)

    at_core = (dp + 1 - 2 * core, mp)
    at_zl = (lax.rem(dp + 8, 16), mp)
    at_zh = (dp, mp + 1 - 2 * zh)

    def remote(name, q, j, src, dst, target):
        column = COLUMNS[name][0] + j
        return pltpu.make_async_remote_copy(
            src_ref=src, dst_ref=dst,
            send_sem=send_sem.at[q, column], recv_sem=recv_sem.at[q, column],
            device_id=target, device_id_type=MESH,
        )

    def mine(q):
        return pl.ds(pl.multiple_of(q * rows, rows), rows)

    def chunk_rows(q):
        return pl.ds(pl.multiple_of(q * height, height), height)

    GROUP = (slice(0, 2), slice(2, 3))
    BACK = (slice(0, 1), slice(1, 3))

    def copies(name, q):
        kind, g = name[:-1], None
        if name[-1] in "01":
            g = int(name[-1])
        if name == "tok_z":
            return [remote(name, q, 0, tokens.at[mine(q)], tok.at[q, y, zh], at_zh)]
        if name == "cot_y":
            return [remote(name, q, k - 1, cotangent.at[mine(q)], cot.at[q, y, zh], at_y(k)) for k in (1, 3, 2)]
        if name == "tok_y":
            return [remote(name, q, k - 1, tok.at[q, y], tok.at[q, y], at_y(k)) for k in (1, 3, 2)]
        if name == "cot_z":
            return [remote(name, q, 0, cot.at[q, :, zh], cot.at[q, :, zh], at_zh)]
        if kind == "core":
            return [remote(name, q, 0, part.at[lax.rem(q, 2), GROUP[g], 1 - core], crecv.at[q, GROUP[g]], at_core)]
        if kind == "x":
            return [remote(name, q, k - 1, xs.at[q, GROUP[g], lax.rem(x + k, 4)], xr.at[q, k - 1, GROUP[g]], at_x(k)) for k in (1, 3, 2)]
        if kind == "z":
            return [remote(name, q, 0, xown.at[q, GROUP[g], 1 - zl], zr.at[q, GROUP[g]], at_zl)]
        if kind == "back_z":
            ref = full.at[q, BACK[g], core, x, zl]
            return [remote(name, q, 0, ref, ref, at_zl)]
        if kind == "back_x":
            ref = full.at[q, BACK[g], core, x]
            return [remote(name, q, k - 1, ref, ref, at_x(k)) for k in (1, 3, 2)]
        if kind == "back_c":
            ref = full.at[q, BACK[g], core]
            return [remote(name, q, 0, ref, ref, at_core)]
        if name == "mix_y":
            return [remote(name, q, k - 1, ms.at[q, lax.rem(y + k, 4)], mr.at[q, k - 1], at_y(k)) for k in (1, 3, 2)]
        if name == "mix_z":
            return [remote(name, q, 0, mz.at[q], mzr.at[q], at_zh)]
        if name == "gt_z":
            return [remote(name, q, 0, gs.at[q, :, 1 - zh], gr.at[q], at_zh)]
        if name == "gt_y":
            return [remote(name, q, k - 1, gys.at[q, lax.rem(y + k, 4)], gyr.at[q, k - 1], at_y(k)) for k in (1, 3, 2)]

    def start(name, q):
        for copy in copies(name, q):
            copy.start()

    def arrived(name, q):
        for copy in copies(name, q):
            copy.wait_recv()

    def sent(name, q):
        for copy in copies(name, q):
            copy.wait_send()

    def own_copies(q):
        return [
            pltpu.make_async_copy(tokens.at[mine(q)], tok.at[q, y, zh], own_sem.at[q, 0]),
            pltpu.make_async_copy(cotangent.at[mine(q)], cot.at[q, y, zh], own_sem.at[q, 1]),
        ]

    loads = [
        pltpu.make_async_copy(gate_w, gw, load_sem.at[0]),
        pltpu.make_async_copy(up_w, uw, load_sem.at[1]),
        pltpu.make_async_copy(down_w, dw, load_sem.at[2]),
    ]

    def out_copy(q, i):
        src = (tok.at[q], cot.at[q], full.at[q, 0], full.at[q, 1], full.at[q, 2])[i]
        dst = (tok_out, cot_out, hid_out, ggp_out, gup_out)[i].at[q]
        return pltpu.make_async_copy(src, dst, out_sem.at[q, i])

    def a0(q):
        start("tok_z", q)
        start("cot_y", q)

    def a1(q):
        for copy in own_copies(q):
            copy.wait()
        arrived("tok_z", q)
        start("tok_y", q)
        arrived("cot_y", q)
        start("cot_z", q)

    def g1a(q):
        arrived("tok_y", q)
        out_copy(q, 0).start()
        block = tok[q].reshape(height, 1152)
        slot = lax.rem(q, 2)

        @pl.loop(0, 4)
        def _(n):
            cols = pl.ds(pl.multiple_of(n * 256, 256), 256)
            part[slot, 0, :, :, cols] = dot(block, gw[:, cols]).reshape(2, height // 2, 256)
            part[slot, 1, :, :, cols] = dot(block, uw[:, cols]).reshape(2, height // 2, 256)

        start("core0", q)

    def g1b(q):
        arrived("cot_z", q)
        out_copy(q, 1).start()
        block = cot[q].reshape(height, 1152)
        slot = lax.rem(q, 2)

        @pl.loop(0, 4)
        def _(n):
            cols = pl.ds(pl.multiple_of(n * 256, 256), 256)
            part[slot, 2, :, :, cols] = dot_t(block, dw[cols, :]).reshape(2, height // 2, 256)

        start("core1", q)

    def b1(q, g):
        arrived(f"core{g}", q)
        sent(f"core{g}", q)
        slot = lax.rem(q, 2)
        for i in range(*((0, 2), (2, 3))[g]):
            total = part[slot, i, core] + crecv[q, i]
            part[slot, i, core] = total
            xs[q, i] = total.astype(BF16).reshape(4, 2, share, 1024)
            own = pl.ds(pl.multiple_of(x * 2 * share, 2 * share), 2 * share)
            xown[q, i] = part[slot, i, core, own].reshape(2, share, 1024)
        start(f"x{g}", q)

    def b2(q, g):
        arrived(f"x{g}", q)
        for i in range(*((0, 2), (2, 3))[g]):
            xown[q, i] = (
                xown[q, i] + xr[q, 0, i].astype(F32) + xr[q, 1, i].astype(F32) + xr[q, 2, i].astype(F32)
            )
        start(f"z{g}", q)

    def e_a(q):
        arrived("z0", q)
        gate = xown[q, 0, zl] + zr[q, 0]
        up = xown[q, 1, zl] + zr[q, 1]
        zr[q, 0] = gate
        zr[q, 1] = up
        sigma = jax.nn.sigmoid(gate)
        full[q, 0, core, x, zl] = (gate * sigma * up).astype(BF16)
        start("back_z0", q)

    def e_b(q):
        arrived("z1", q)
        gate = zr[q, 0]
        up = zr[q, 1]
        sigma = jax.nn.sigmoid(gate)
        grad = xown[q, 2, zl] + zr[q, 2]
        full[q, 1, core, x, zl] = (grad * up * sigma * (1.0 + gate * (1.0 - sigma))).astype(BF16)
        full[q, 2, core, x, zl] = (grad * gate * sigma).astype(BF16)
        start("back_z1", q)

    def c1(q, g):
        arrived(f"back_z{g}", q)
        start(f"back_x{g}", q)

    def c2(q, g):
        arrived(f"back_x{g}", q)
        start(f"back_c{g}", q)

    def g2a(q):
        arrived("back_c0", q)
        out_copy(q, 2).start()
        block = full[q, 0].reshape(height, 1024)

        @pl.loop(0, 3)
        def _(n):
            cols = pl.ds(pl.multiple_of(n * 384, 384), 384)
            tmp[:, :, :, cols] = dot(block, dw[:, cols]).reshape(4, 2, rows, 384)

        ms[q] = tmp[...].astype(BF16)
        mown[q] = tmp[y]
        start("mix_y", q)

    def g2b(q):
        arrived("back_c1", q)
        out_copy(q, 3).start()
        out_copy(q, 4).start()
        left = full[q, 1].reshape(height, 1024)
        right = full[q, 2].reshape(height, 1024)

        @pl.loop(0, 3)
        def _(n):
            cols = pl.ds(pl.multiple_of(n * 384, 384), 384)
            tmp[:, :, :, cols] = (dot_t(left, gw[cols, :]) + dot_t(right, uw[cols, :])).reshape(4, 2, rows, 384)

        gs[q] = tmp[...].astype(BF16)
        gown[q] = tmp[:, zh]
        start("gt_z", q)

    def d1a(q):
        arrived("mix_y", q)
        mown[q] = mown[q] + mr[q, 0].astype(F32) + mr[q, 1].astype(F32) + mr[q, 2].astype(F32)
        mz[q] = mown[q, 1 - zh].astype(BF16)
        start("mix_z", q)

    def d1b(q):
        arrived("gt_z", q)
        total = gown[q] + gr[q].astype(F32)
        gown[q] = total
        gys[q] = total.astype(BF16)
        start("gt_y", q)

    def d2a(q):
        arrived("mix_z", q)
        mixed[mine(q), :] = (mown[q, zh] + mzr[q].astype(F32)).astype(BF16)

    def d2b(q):
        arrived("gt_y", q)
        grad_tokens[mine(q), :] = (
            gown[q, y] + gyr[q, 0].astype(F32) + gyr[q, 1].astype(F32) + gyr[q, 2].astype(F32)
        ).astype(BF16)

    for copy in loads:
        copy.start()
    peers = [at_core, at_zl, at_zh] + [at_x(k) for k in (1, 2, 3)] + [at_y(k) for k in (1, 2, 3)]
    barrier = pltpu.get_barrier_semaphore()
    for peer in peers:
        pl.semaphore_signal(barrier, inc=1, device_id=peer, device_id_type=MESH)
    for q in range(CHUNKS):
        for copy in own_copies(q):
            copy.start()
    pl.semaphore_wait(barrier, len(peers))
    a0(0)
    for copy in loads:
        copy.wait()

    plan = PLAN(locals())
    ticks = CHUNKS + max(delay for _, delay in plan)

    @pl.loop(0, ticks)
    def _(t):
        for stage, delay in plan:
            q = t - delay

            @pl.when(jnp.logical_and(q >= 0, q < CHUNKS))
            def _():
                stage(q)

    @pl.loop(0, CHUNKS)
    def _(q):
        for name in COLUMNS:
            if not name.startswith("core"):
                sent(name, q)
        for i in range(5):
            out_copy(q, i).wait()


def PLAN(s):
    b1, b2, c1, c2 = s["b1"], s["b2"], s["c1"], s["c2"]

    def next_a0(q):
        @pl.when(q + 1 < CHUNKS)
        def _():
            s["a0"](q + 1)

    return [
        (s["e_a"], 2), (s["e_b"], 2),
        (lambda q: b1(q, 0), 1), (lambda q: b1(q, 1), 1),
        (s["g2a"], 3), (s["g2b"], 3),
        (lambda q: c1(q, 0), 2), (lambda q: c1(q, 1), 2),
        (s["a1"], 0), (next_a0, 0),
        (lambda q: b2(q, 0), 1), (lambda q: b2(q, 1), 1),
        (s["d1a"], 3), (s["d1b"], 3),
        (s["g1a"], 0), (s["g1b"], 0),
        (lambda q: c2(q, 0), 2), (lambda q: c2(q, 1), 2),
        (s["d2a"], 3), (s["d2b"], 3),
    ]


def block(tokens, gate_weight, up_weight, down_weight, cotangent):
    n = CHUNKS
    rows, height = 128 // n, 1024 // n
    share = height // 16
    anyspace = pl.BlockSpec(memory_space=pl.ANY)
    vmem = pl.BlockSpec(memory_space=pltpu.VMEM)
    out_shape = [
        jax.ShapeDtypeStruct((128, 1152), BF16),
        jax.ShapeDtypeStruct((128, 1152), BF16),
        jax.ShapeDtypeStruct((n, Y, 2, rows, 1152), BF16),
        jax.ShapeDtypeStruct((n, Y, 2, rows, 1152), BF16),
        jax.ShapeDtypeStruct((n, 2, X, 2, share, 1024), BF16),
        jax.ShapeDtypeStruct((n, 2, X, 2, share, 1024), BF16),
        jax.ShapeDtypeStruct((n, 2, X, 2, share, 1024), BF16),
    ]
    V = pltpu.VMEM
    scratch = [
        V((1152, 1024), BF16), V((1152, 1024), BF16), V((1024, 1152), BF16),
        V((n, Y, 2, rows, 1152), BF16), V((n, Y, 2, rows, 1152), BF16),
        V((2, 3, 2, height // 2, 1024), F32), V((n, 3, height // 2, 1024), F32),
        V((n, 3, X, 2, share, 1024), BF16), V((n, 3, 3, 2, share, 1024), BF16),
        V((n, 3, 2, share, 1024), F32), V((n, 3, share, 1024), F32),
        V((n, 3, 2, X, 2, share, 1024), BF16),
        V((Y, 2, rows, 1152), F32),
        V((n, Y, 2, rows, 1152), BF16), V((n, 2, rows, 1152), F32), V((n, 3, 2, rows, 1152), BF16),
        V((n, rows, 1152), BF16), V((n, rows, 1152), BF16),
        V((n, Y, 2, rows, 1152), BF16), V((n, Y, rows, 1152), F32), V((n, Y, rows, 1152), BF16),
        V((n, Y, rows, 1152), BF16), V((n, 3, rows, 1152), BF16),
        pltpu.SemaphoreType.DMA((n, TOTAL)), pltpu.SemaphoreType.DMA((n, TOTAL)),
        pltpu.SemaphoreType.DMA((3,)), pltpu.SemaphoreType.DMA((n, 2)), pltpu.SemaphoreType.DMA((n, 5)),
    ]
    return pl.pallas_call(
        kernel,
        out_shape=out_shape,
        in_specs=[anyspace] * 5,
        out_specs=[vmem, vmem] + [anyspace] * 5,
        scratch_shapes=scratch,
        compiler_params=pltpu.CompilerParams(
            collective_id=0, has_side_effects=True, vmem_limit_bytes=62 << 20
        ),
        cost_estimate=pl.CostEstimate(flops=14_500_000_000, bytes_accessed=30_000_000, transcendentals=0),
        name="exchange",
    )(tokens, gate_weight, up_weight, down_weight, cotangent)


def on_device(tokens, gate_weight, up_weight, down_weight, cotangent):
    mixed, grad_tokens, rows_all, cot_all, hidden, ggp, gup = block(
        tokens, gate_weight, up_weight, down_weight, cotangent
    )
    rows_all = rows_all.reshape(1024, 1152)
    cot_all = cot_all.reshape(1024, 1152)
    hidden, ggp, gup = (a.reshape(1024, 1024) for a in (hidden, ggp, gup))
    grad_gate = inner_rows(rows_all, ggp)
    grad_up = inner_rows(rows_all, gup)
    grad_down = inner_rows(hidden, cot_all)
    return (mixed, grad_tokens, grad_gate, grad_up, grad_down)


def solution(mesh):
    in_specs = (P("mp", "dp"), P("dp", "mp"), P("dp", "mp"), P("mp", "dp"), P("mp", "dp"))
    out_specs = (P("mp", "dp"), P("mp", "dp"), P("dp", "mp"), P("dp", "mp"), P("mp", "dp"))
    return jax.shard_map(
        on_device, mesh=mesh, in_specs=in_specs, out_specs=out_specs, check_vma=False
    )
```

```python
import functools

import jax
import jax.numpy as jnp
from jax import lax
from jax.experimental import pallas as pl
from jax.experimental.pallas import tpu as pltpu
from jax.sharding import PartitionSpec as P

MESH = pl.DeviceIdType.MESH
F32 = jnp.float32
BF16 = jnp.bfloat16
CHUNKS = 4
Y, X = 4, 4


def dot(left, right):
    return lax.dot_general(left, right, (((1,), (0,)), ((), ())), preferred_element_type=F32)


def dot_t(left, right):
    return lax.dot_general(left, right, (((1,), (1,)), ((), ())), preferred_element_type=F32)


def inner_rows(left, right):
    return lax.dot_general(left, right, (((0,), (0,)), ((), ())), preferred_element_type=F32)


COLUMNS = {}
for name, copies in (
    ("tok_z", 1), ("cot_y", 3), ("tok_y", 3), ("cot_z", 1),
    ("core0", 1), ("core1", 1), ("x0", 3), ("x1", 3), ("z0", 1), ("z1", 1),
    ("back_x0", 2), ("back_x1", 2), ("pass_x0", 2), ("pass_x1", 2), ("back_c0", 1), ("back_c1", 1),
    ("mix_y", 3), ("mix_z", 1), ("gt_z", 1), ("gt_y", 3),
):
    COLUMNS[name] = (sum(n for _, n in COLUMNS.values()), copies)
TOTAL = sum(n for _, n in COLUMNS.values())


def kernel(
    tokens, gate_w, up_w, down_w, cotangent,
    mixed, grad_tokens, tok_out, cot_out, hid_out, ggp_out, gup_out,
    gw, uw, dw, tok, cot, part, crecv, xs, xr, xown, zs, zr, full, tmp,
    ms, mown, mr, mz, mzr, gs, gown, gr, gys, gyr,
    send_sem, recv_sem, load_sem, own_sem, out_sem,
):
    rows = 128 // CHUNKS
    height = 1024 // CHUNKS
    share = height // 8
    dp, mp = lax.axis_index("dp"), lax.axis_index("mp")
    core = lax.rem(dp, 2)
    x = lax.rem(dp // 2, 4)
    zl = dp // 8
    y = mp // 2
    zh = lax.rem(mp, 2)

    def at_x(k):
        return (zl * 8 + lax.rem(x + k, 4) * 2 + core, mp)

    def at_y(k):
        return (dp, lax.rem(y + k, 4) * 2 + zh)

    at_core = (dp + 1 - 2 * core, mp)
    at_zl = (lax.rem(dp + 8, 16), mp)
    at_zh = (dp, mp + 1 - 2 * zh)

    def remote(name, q, j, src, dst, target):
        column = COLUMNS[name][0] + j
        return pltpu.make_async_remote_copy(
            src_ref=src, dst_ref=dst,
            send_sem=send_sem.at[q, column], recv_sem=recv_sem.at[q, column],
            device_id=target, device_id_type=MESH,
        )

    def mine(q):
        return pl.ds(pl.multiple_of(q * rows, rows), rows)

    def chunk_rows(q):
        return pl.ds(pl.multiple_of(q * height, height), height)

    GROUP = (slice(0, 2), slice(2, 3))
    BACK = (slice(0, 1), slice(1, 3))

    def copies(name, q):
        kind, g = name[:-1], None
        if name[-1] in "01":
            g = int(name[-1])
        if name == "tok_z":
            return [remote(name, q, 0, tokens.at[mine(q)], tok.at[q, y, zh], at_zh)]
        if name == "cot_y":
            return [remote(name, q, k - 1, cotangent.at[mine(q)], cot.at[q, y, zh], at_y(k)) for k in (1, 3, 2)]
        if name == "tok_y":
            return [remote(name, q, k - 1, tok.at[q, y], tok.at[q, y], at_y(k)) for k in (1, 3, 2)]
        if name == "cot_z":
            return [remote(name, q, 0, cot.at[q, :, zh], cot.at[q, :, zh], at_zh)]
        if kind == "core":
            return [remote(name, q, 0, part.at[q, GROUP[g], 1 - core], crecv.at[q, GROUP[g]], at_core)]
        if kind == "x":
            return [remote(name, q, k - 1, xs.at[q, GROUP[g], lax.rem(x + k, 4)], xr.at[q, k - 1, GROUP[g]], at_x(k)) for k in (1, 3, 2)]
        if kind == "z":
            return [remote(name, q, 0, zs.at[q, GROUP[g]], zr.at[q, GROUP[g]], at_zl)]
        if kind == "back_x":
            ref = full.at[q, BACK[g], core, x]
            return [remote(name, q, i, ref, ref, at_x(k)) for i, k in enumerate((1, 3))]
        if kind == "pass_x":
            result = []
            for i, k in enumerate((1, 3)):
                ref = full.at[q, BACK[g], core, lax.rem(x + 4 - k, 4), :, pl.ds(i * 512, 512)]
                result.append(remote(name, q, i, ref, ref, at_x(k)))
            return result
        if kind == "back_c":
            ref = full.at[q, BACK[g], core]
            return [remote(name, q, 0, ref, ref, at_core)]
        if name == "mix_y":
            return [remote(name, q, k - 1, ms.at[q, lax.rem(y + k, 4)], mr.at[q, k - 1], at_y(k)) for k in (1, 3, 2)]
        if name == "mix_z":
            return [remote(name, q, 0, mz.at[q], mzr.at[q], at_zh)]
        if name == "gt_z":
            return [remote(name, q, 0, gs.at[q, :, 1 - zh], gr.at[q], at_zh)]
        if name == "gt_y":
            return [remote(name, q, k - 1, gys.at[q, lax.rem(y + k, 4)], gyr.at[q, k - 1], at_y(k)) for k in (1, 3, 2)]

    def start(name, q):
        for copy in copies(name, q):
            copy.start()

    def arrived(name, q):
        for copy in copies(name, q):
            copy.wait_recv()

    def sent(name, q):
        for copy in copies(name, q):
            copy.wait_send()

    def own_copy(q, i):
        src, dst = ((tokens, tok), (cotangent, cot))[i]
        return pltpu.make_async_copy(src.at[mine(q)], dst.at[q, y, zh], own_sem.at[q, i])

    def load(i):
        src, dst = ((gate_w, gw), (up_w, uw), (down_w, dw))[i]
        return pltpu.make_async_copy(src, dst, load_sem.at[i])

    def out_copy(q, i):
        src = (tok.at[q], cot.at[q], full.at[q, 0], full.at[q, 1], full.at[q, 2])[i]
        dst = (tok_out, cot_out, hid_out, ggp_out, gup_out)[i].at[q]
        return pltpu.make_async_copy(src, dst, out_sem.at[q, i])

    def a0(q):
        start("tok_z", q)
        start("cot_y", q)

    def a1t(q):
        own_copy(q, 0).wait()
        arrived("tok_z", q)
        start("tok_y", q)

    def a1c(q):
        own_copy(q, 1).wait()
        arrived("cot_y", q)
        start("cot_z", q)

    def g1a(q):
        arrived("tok_y", q)
        if q == 0:
            load(0).wait()
            load(1).wait()
        out_copy(q, 0).start()
        block = tok[q].reshape(height, 1152)
        slot = q

        @pl.loop(0, 4)
        def _(n):
            cols = pl.ds(pl.multiple_of(n * 256, 256), 256)
            part[slot, 0, :, :, cols] = dot(block, gw[:, cols]).reshape(2, height // 2, 256)
            part[slot, 1, :, :, cols] = dot(block, uw[:, cols]).reshape(2, height // 2, 256)

        start("core0", q)

    def g1b(q):
        arrived("cot_z", q)
        if q == 0:
            load(2).wait()
        out_copy(q, 1).start()
        block = cot[q].reshape(height, 1152)
        slot = q

        @pl.loop(0, 4)
        def _(n):
            cols = pl.ds(pl.multiple_of(n * 256, 256), 256)
            part[slot, 2, :, :, cols] = dot_t(block, dw[cols, :]).reshape(2, height // 2, 256)

        start("core1", q)

    def b1(q, g):
        arrived(f"core{g}", q)
        sent(f"core{g}", q)
        for i in range(*((0, 2), (2, 3))[g]):
            total = part[q, i, core] + crecv[q, i]
            xs[q, i] = total.astype(BF16).reshape(X, share, 1024)
            own = pl.ds(pl.multiple_of(x * share, share), share)
            xown[q, i] = part[q, i, core, own] + crecv[q, i, own]
        start(f"x{g}", q)

    def b2(q, g):
        arrived(f"x{g}", q)
        for i in range(*((0, 2), (2, 3))[g]):
            total = xown[q, i] + xr[q, 0, i].astype(F32) + xr[q, 1, i].astype(F32) + xr[q, 2, i].astype(F32)
            xown[q, i] = total
            zs[q, i] = total.astype(BF16)
        start(f"z{g}", q)

    def summed(q, i):
        return xown[q, i] + zr[q, i].astype(F32)

    def e_a(q):
        arrived("z0", q)
        gate, up = summed(q, 0), summed(q, 1)
        full[q, 0, core, x] = (gate * jax.nn.sigmoid(gate) * up).astype(BF16)
        start("back_x0", q)

    def e_b(q):
        arrived("z1", q)
        gate, up, grad = summed(q, 0), summed(q, 1), summed(q, 2)
        sigma = jax.nn.sigmoid(gate)
        full[q, 1, core, x] = (grad * up * sigma * (1.0 + gate * (1.0 - sigma))).astype(BF16)
        full[q, 2, core, x] = (grad * gate * sigma).astype(BF16)
        start("back_x1", q)

    def c1(q, g):
        arrived(f"back_x{g}", q)
        start(f"pass_x{g}", q)

    def c2(q, g):
        arrived(f"pass_x{g}", q)
        start(f"back_c{g}", q)

    def g2a(q):
        arrived("back_c0", q)
        out_copy(q, 2).start()
        block = full[q, 0].reshape(height, 1024)

        @pl.loop(0, 3)
        def _(n):
            cols = pl.ds(pl.multiple_of(n * 384, 384), 384)
            tmp[:, :, :, cols] = dot(block, dw[:, cols]).reshape(4, 2, rows, 384)

        ms[q] = tmp[...].astype(BF16)
        mown[q] = tmp[y]
        start("mix_y", q)

    def g2b(q):
        arrived("back_c1", q)
        out_copy(q, 3).start()
        out_copy(q, 4).start()
        left = full[q, 1].reshape(height, 1024)
        right = full[q, 2].reshape(height, 1024)

        @pl.loop(0, 3)
        def _(n):
            cols = pl.ds(pl.multiple_of(n * 384, 384), 384)
            tmp[:, :, :, cols] = (dot_t(left, gw[cols, :]) + dot_t(right, uw[cols, :])).reshape(4, 2, rows, 384)

        gs[q] = tmp[...].astype(BF16)
        gown[q] = tmp[:, zh]
        start("gt_z", q)

    def d1a(q):
        arrived("mix_y", q)
        mown[q] = mown[q] + mr[q, 0].astype(F32) + mr[q, 1].astype(F32) + mr[q, 2].astype(F32)
        mz[q] = mown[q, 1 - zh].astype(BF16)
        start("mix_z", q)

    def d1b(q):
        arrived("gt_z", q)
        total = gown[q] + gr[q].astype(F32)
        gown[q] = total
        gys[q] = total.astype(BF16)
        start("gt_y", q)

    def d2a(q):
        arrived("mix_z", q)
        mixed[mine(q), :] = (mown[q, zh] + mzr[q].astype(F32)).astype(BF16)

    def d2b(q):
        arrived("gt_y", q)
        grad_tokens[mine(q), :] = (
            gown[q, y] + gyr[q, 0].astype(F32) + gyr[q, 1].astype(F32) + gyr[q, 2].astype(F32)
        ).astype(BF16)

    stages = dict(
        a0=a0, a1t=a1t, a1c=a1c, g1a=g1a, g1b=g1b,
        b1a=lambda q: b1(q, 0), b1b=lambda q: b1(q, 1),
        b2a=lambda q: b2(q, 0), b2b=lambda q: b2(q, 1),
        ea=e_a, eb=e_b,
        c15a=lambda q: c1(q, 0), c15b=lambda q: c1(q, 1),
        c2a=lambda q: c2(q, 0), c2b=lambda q: c2(q, 1),
        g2a=g2a, g2b=g2b, d1a=d1a, d1b=d1b, d2a=d2a, d2b=d2b,
    )

    for i in range(3):
        load(i).start()
    peers = [at_core, at_zl, at_zh] + [at_x(k) for k in (1, 2, 3)] + [at_y(k) for k in (1, 2, 3)]
    barrier = pltpu.get_barrier_semaphore()
    for peer in peers:
        pl.semaphore_signal(barrier, inc=1, device_id=peer, device_id_type=MESH)
    for q in range(CHUNKS):
        own_copy(q, 0).start()
        own_copy(q, 1).start()
    pl.semaphore_wait(barrier, len(peers))

    for stage, q in PLAN:
        stages[stage](q)

    @pl.loop(0, CHUNKS)
    def _(q):
        for name in COLUMNS:
            if not name.startswith("core"):
                sent(name, q)
        for i in range(5):
            out_copy(q, i).wait()


PLAN = (
    ("a0", 0), ("a1t", 0), ("a0", 2), ("a1c", 0), ("a1t", 2), ("g1a", 0), ("a0", 1), ("a1c", 2),
    ("b1a", 0), ("g1b", 0), ("a0", 3), ("a1t", 1), ("b1b", 0), ("g1a", 2), ("g1b", 2), ("b2a", 0),
    ("b1a", 2), ("b2b", 0), ("ea", 0), ("a1c", 1), ("eb", 0), ("b1b", 2), ("g1a", 1), ("a1t", 3),
    ("a1c", 3), ("b1a", 1), ("b2a", 2), ("c15a", 0), ("g1b", 1), ("b2b", 2), ("c15b", 0), ("b1b", 1),
    ("b2a", 1), ("g1a", 3), ("c2b", 0), ("ea", 2), ("c2a", 0), ("eb", 2), ("ea", 1), ("g2b", 0),
    ("g1b", 3), ("c15a", 2), ("b1a", 3), ("c15b", 2), ("b1b", 3), ("g2a", 0), ("b2b", 1), ("c2a", 2),
    ("g2a", 2), ("eb", 1), ("b2a", 3), ("c15a", 1), ("d1b", 0), ("c2b", 2), ("d1a", 0), ("ea", 3),
    ("b2b", 3), ("g2b", 2), ("c15b", 1), ("c2a", 1), ("eb", 3), ("g2a", 1), ("c15a", 3), ("c2b", 1),
    ("d1a", 2), ("c15b", 3), ("g2b", 1), ("d1b", 2), ("d2a", 0), ("c2a", 3), ("c2b", 3), ("g2a", 3),
    ("g2b", 3), ("d2b", 0), ("d1b", 1), ("d1a", 3), ("d1a", 1), ("d1b", 3), ("d2a", 2), ("d2b", 2),
    ("d2a", 1), ("d2a", 3), ("d2b", 1), ("d2b", 3),
)


def block(tokens, gate_weight, up_weight, down_weight, cotangent):
    n = CHUNKS
    rows, height = 128 // n, 1024 // n
    share = height // 8
    anyspace = pl.BlockSpec(memory_space=pl.ANY)
    vmem = pl.BlockSpec(memory_space=pltpu.VMEM)
    out_shape = [
        jax.ShapeDtypeStruct((128, 1152), BF16),
        jax.ShapeDtypeStruct((128, 1152), BF16),
        jax.ShapeDtypeStruct((n, Y, 2, rows, 1152), BF16),
        jax.ShapeDtypeStruct((n, Y, 2, rows, 1152), BF16),
        jax.ShapeDtypeStruct((n, 2, X, share, 1024), BF16),
        jax.ShapeDtypeStruct((n, 2, X, share, 1024), BF16),
        jax.ShapeDtypeStruct((n, 2, X, share, 1024), BF16),
    ]
    V = pltpu.VMEM
    scratch = [
        V((1152, 1024), BF16), V((1152, 1024), BF16), V((1024, 1152), BF16),
        V((n, Y, 2, rows, 1152), BF16), V((n, Y, 2, rows, 1152), BF16),
        V((n, 3, 2, height // 2, 1024), F32), V((n, 3, height // 2, 1024), F32),
        V((n, 3, X, share, 1024), BF16), V((n, 3, 3, share, 1024), BF16),
        V((n, 3, share, 1024), F32), V((n, 3, share, 1024), BF16), V((n, 3, share, 1024), BF16),
        V((n, 3, 2, X, share, 1024), BF16),
        V((Y, 2, rows, 1152), F32),
        V((n, Y, 2, rows, 1152), BF16), V((n, 2, rows, 1152), F32), V((n, 3, 2, rows, 1152), BF16),
        V((n, rows, 1152), BF16), V((n, rows, 1152), BF16),
        V((n, Y, 2, rows, 1152), BF16), V((n, Y, rows, 1152), F32), V((n, Y, rows, 1152), BF16),
        V((n, Y, rows, 1152), BF16), V((n, 3, rows, 1152), BF16),
        pltpu.SemaphoreType.DMA((n, TOTAL)), pltpu.SemaphoreType.DMA((n, TOTAL)),
        pltpu.SemaphoreType.DMA((3,)), pltpu.SemaphoreType.DMA((n, 2)), pltpu.SemaphoreType.DMA((n, 5)),
    ]
    return pl.pallas_call(
        kernel,
        out_shape=out_shape,
        in_specs=[anyspace] * 5,
        out_specs=[vmem, vmem] + [anyspace] * 5,
        scratch_shapes=scratch,
        compiler_params=pltpu.CompilerParams(
            collective_id=0, has_side_effects=True, vmem_limit_bytes=63 << 20
        ),
        cost_estimate=pl.CostEstimate(flops=14_500_000_000, bytes_accessed=30_000_000, transcendentals=0),
        name="exchange",
    )(tokens, gate_weight, up_weight, down_weight, cotangent)


def gradients_kernel(
    tok, cot, hid, ggp, gup, grad_gate, grad_up, grad_down,
    tok_v, cot_v, hid_v, ggp_v, gup_v, gate_v, up_v, down_v, in_sem, out_sem,
):
    pairs = ((tok, tok_v), (ggp, ggp_v), (gup, gup_v), (hid, hid_v), (cot, cot_v))
    loads = [pltpu.make_async_copy(src, dst, in_sem.at[i]) for i, (src, dst) in enumerate(pairs)]
    loads[0].start()
    loads[1].start()

    def product(left, right, total, out, height, group):
        def write(m):
            part = pl.ds(pl.multiple_of(m * height, height), height)
            return pltpu.make_async_copy(total.at[part], out.at[part], out_sem.at[group, m])

        tiles = left.shape[1] // height

        @pl.loop(0, tiles)
        def _(m):
            part = pl.ds(pl.multiple_of(m * height, height), height)
            total[part, :] = inner_rows(left[:, part], right[...])
            write(m).start()

        return [write(m) for m in range(tiles)]

    loads[0].wait()
    loads[1].wait()
    for copy in loads[2:]:
        copy.start()
    writes = product(tok_v, ggp_v, gate_v, grad_gate, TILE_A, 0)
    loads[2].wait()
    writes += product(tok_v, gup_v, up_v, grad_up, TILE_A, 1)
    loads[3].wait()
    loads[4].wait()
    writes += product(hid_v, cot_v, down_v, grad_down, TILE_B, 2)
    for copy in writes:
        copy.wait()


TILE_A, TILE_B = 384, 256


def weight_gradients(rows_all, cot_all, hidden, ggp, gup):
    wide, tall = (1024, 1152), (1152, 1024)
    square = (1024, 1024)
    V = pltpu.VMEM
    anyspace = pl.BlockSpec(memory_space=pl.ANY)
    return pl.pallas_call(
        gradients_kernel,
        out_shape=[jax.ShapeDtypeStruct(s, F32) for s in (tall, tall, wide)],
        in_specs=[anyspace] * 5,
        out_specs=[anyspace] * 3,
        scratch_shapes=[
            V(wide, BF16), V(wide, BF16), V(square, BF16), V(square, BF16), V(square, BF16),
            V(tall, F32), V(tall, F32), V(wide, F32),
            pltpu.SemaphoreType.DMA((5,)), pltpu.SemaphoreType.DMA((3, 8)),
        ],
        compiler_params=pltpu.CompilerParams(vmem_limit_bytes=63 << 20),
        cost_estimate=pl.CostEstimate(flops=7_250_000_000, bytes_accessed=25_000_000, transcendentals=0),
        name="weight_gradients",
    )(rows_all, cot_all, hidden, ggp, gup)


def on_device(tokens, gate_weight, up_weight, down_weight, cotangent):
    mixed, grad_tokens, rows_all, cot_all, hidden, ggp, gup = block(
        tokens, gate_weight, up_weight, down_weight, cotangent
    )
    rows_all = rows_all.reshape(1024, 1152)
    cot_all = cot_all.reshape(1024, 1152)
    hidden, ggp, gup = (a.reshape(1024, 1024) for a in (hidden, ggp, gup))
    grad_gate, grad_up, grad_down = weight_gradients(rows_all, cot_all, hidden, ggp, gup)
    return (mixed, grad_tokens, grad_gate, grad_up, grad_down)


def solution(mesh):
    in_specs = (P("mp", "dp"), P("dp", "mp"), P("dp", "mp"), P("mp", "dp"), P("mp", "dp"))
    out_specs = (P("mp", "dp"), P("mp", "dp"), P("dp", "mp"), P("dp", "mp"), P("mp", "dp"))
    return jax.shard_map(
        on_device, mesh=mesh, in_specs=in_specs, out_specs=out_specs, check_vma=False
    )
```

```python
import functools

import jax
import jax.numpy as jnp
from jax import lax
from jax.experimental import pallas as pl
from jax.experimental.pallas import tpu as pltpu
from jax.sharding import PartitionSpec as P

MESH = pl.DeviceIdType.MESH
F32 = jnp.float32
BF16 = jnp.bfloat16
CHUNKS = 4
Y, X = 4, 4


def dot(left, right):
    return lax.dot_general(left, right, (((1,), (0,)), ((), ())), preferred_element_type=F32)


def dot_t(left, right):
    return lax.dot_general(left, right, (((1,), (1,)), ((), ())), preferred_element_type=F32)


def inner_rows(left, right):
    return lax.dot_general(left, right, (((0,), (0,)), ((), ())), preferred_element_type=F32)


COLUMNS = {}
for name, copies in (
    ("tok_z", 1), ("cot_y", 3), ("tok_y", 3), ("cot_z", 1),
    ("core0", 1), ("core1", 1), ("x0", 3), ("x1", 3), ("z0", 1), ("z1", 1),
    ("back_x0", 2), ("back_x1", 2), ("pass_x0", 2), ("pass_x1", 2), ("back_c0", 1), ("back_c1", 1),
    ("mix_y", 3), ("mix_z", 1), ("gt_z", 1), ("gt_y", 3),
):
    COLUMNS[name] = (sum(n for _, n in COLUMNS.values()), copies)
TOTAL = sum(n for _, n in COLUMNS.values())


def kernel(
    tokens, gate_w, up_w, down_w, cotangent,
    mixed, grad_tokens, tok_out, cot_out, hid_out, ggp_out, gup_out,
    gw, uw, dw, tok, cot, part, crecv, xs, xr, xown, zr, full, tmp, tok_t, hid_t,
    ms, mown, mr, mz, mzr, gs, gown, gr, gys, gyr,
    send_sem, recv_sem, load_sem, own_sem, out_sem,
):
    rows = 128 // CHUNKS
    height = 1024 // CHUNKS
    share = height // 8
    dp, mp = lax.axis_index("dp"), lax.axis_index("mp")
    core = lax.rem(dp, 2)
    x = lax.rem(dp // 2, 4)
    zl = dp // 8
    y = mp // 2
    zh = lax.rem(mp, 2)

    def at_x(k):
        return (zl * 8 + lax.rem(x + k, 4) * 2 + core, mp)

    def at_y(k):
        return (dp, lax.rem(y + k, 4) * 2 + zh)

    at_core = (dp + 1 - 2 * core, mp)
    at_zl = (lax.rem(dp + 8, 16), mp)
    at_zh = (dp, mp + 1 - 2 * zh)

    def remote(name, q, j, src, dst, target):
        column = COLUMNS[name][0] + j
        return pltpu.make_async_remote_copy(
            src_ref=src, dst_ref=dst,
            send_sem=send_sem.at[q, column], recv_sem=recv_sem.at[q, column],
            device_id=target, device_id_type=MESH,
        )

    def mine(q):
        return pl.ds(pl.multiple_of(q * rows, rows), rows)

    def chunk_rows(q):
        return pl.ds(pl.multiple_of(q * height, height), height)

    GROUP = (slice(0, 2), slice(2, 3))
    BACK = (slice(0, 1), slice(1, 3))

    def copies(name, q):
        kind, g = name[:-1], None
        if name[-1] in "01":
            g = int(name[-1])
        if name == "tok_z":
            return [remote(name, q, 0, tokens.at[mine(q)], tok.at[q, y, zh], at_zh)]
        if name == "cot_y":
            return [remote(name, q, k - 1, cotangent.at[mine(q)], cot.at[q, y, zh], at_y(k)) for k in (2, 1, 3)]
        if name == "tok_y":
            return [remote(name, q, k - 1, tok.at[q, y], tok.at[q, y], at_y(k)) for k in (2, 1, 3)]
        if name == "cot_z":
            return [remote(name, q, 0, cot.at[q, :, zh], cot.at[q, :, zh], at_zh)]
        if kind == "core":
            return [remote(name, q, 0, part.at[q, GROUP[g], 1 - core], crecv.at[q, GROUP[g]], at_core)]
        if kind == "x":
            return [remote(name, q, k - 1, xs.at[q, GROUP[g], lax.rem(x + k, 4)], xr.at[q, k - 1, GROUP[g]], at_x(k)) for k in (2, 1, 3)]
        if kind == "z":
            return [remote(name, q, 0, xs.at[q, GROUP[g], x], zr.at[q, GROUP[g]], at_zl)]
        if kind == "back_x":
            ref = full.at[q, BACK[g], core, x]
            return [remote(name, q, i, ref, ref, at_x(k)) for i, k in enumerate((1, 3))]
        if kind == "pass_x":
            result = []
            for i, k in enumerate((1, 3)):
                ref = full.at[q, BACK[g], core, lax.rem(x + 4 - k, 4), :, pl.ds(i * 512, 512)]
                result.append(remote(name, q, i, ref, ref, at_x(k)))
            return result
        if kind == "back_c":
            ref = full.at[q, BACK[g], core]
            return [remote(name, q, 0, ref, ref, at_core)]
        if name == "mix_y":
            return [remote(name, q, k - 1, ms.at[q, lax.rem(y + k, 4)], mr.at[q, k - 1], at_y(k)) for k in (2, 1, 3)]
        if name == "mix_z":
            return [remote(name, q, 0, mz.at[q], mzr.at[q], at_zh)]
        if name == "gt_z":
            return [remote(name, q, 0, gs.at[q, :, 1 - zh], gr.at[q], at_zh)]
        if name == "gt_y":
            return [remote(name, q, k - 1, gys.at[q, lax.rem(y + k, 4)], gyr.at[q, k - 1], at_y(k)) for k in (2, 1, 3)]

    def start(name, q):
        for copy in copies(name, q):
            copy.start()

    def arrived(name, q):
        for copy in copies(name, q):
            copy.wait_recv()

    def sent(name, q):
        for copy in copies(name, q):
            copy.wait_send()

    def own_copy(q, i):
        src, dst = ((tokens, tok), (cotangent, cot))[i]
        return pltpu.make_async_copy(src.at[mine(q)], dst.at[q, y, zh], own_sem.at[q, i])

    def load(i):
        src, dst = ((gate_w, gw), (up_w, uw), (down_w, dw))[i]
        return pltpu.make_async_copy(src, dst, load_sem.at[i])

    def out_copy(q, i):
        part = pl.ds(q * height, height)
        src = (tok_t.at[:, part], cot.at[q], hid_t.at[:, part], full.at[q, 1], full.at[q, 2])[i]
        dst = (tok_out.at[:, part], cot_out.at[q], hid_out.at[:, part], ggp_out.at[q], gup_out.at[q])[i]
        return pltpu.make_async_copy(src, dst, out_sem.at[q, i])

    def a0(q):
        start("tok_z", q)
        start("cot_y", q)

    def a1t(q):
        own_copy(q, 0).wait()
        arrived("tok_z", q)
        start("tok_y", q)

    def a1c(q):
        own_copy(q, 1).wait()
        arrived("cot_y", q)
        start("cot_z", q)

    def g1a(q):
        arrived("tok_y", q)
        if q == next(c for stage, c in PLAN if stage == "g1a"):
            load(0).wait()
            load(1).wait()
        block = tok[q].reshape(height, 1152)
        slot = q

        @pl.loop(0, 4)
        def _(n):
            cols = pl.ds(pl.multiple_of(n * 256, 256), 256)
            part[slot, 0, :, :, cols] = dot(block, gw[:, cols]).reshape(2, height // 2, 256)
            part[slot, 1, :, :, cols] = dot(block, uw[:, cols]).reshape(2, height // 2, 256)

        start("core0", q)
        tok_t[:, pl.ds(q * height, height)] = block.T
        out_copy(q, 0).start()

    def g1b(q):
        arrived("cot_z", q)
        if q == next(c for stage, c in PLAN if stage == "g1b"):
            load(2).wait()
        out_copy(q, 1).start()
        block = cot[q].reshape(height, 1152)
        slot = q

        @pl.loop(0, 4)
        def _(n):
            cols = pl.ds(pl.multiple_of(n * 256, 256), 256)
            part[slot, 2, :, :, cols] = dot_t(block, dw[cols, :]).reshape(2, height // 2, 256)

        start("core1", q)

    def b1(q, g):
        arrived(f"core{g}", q)
        sent(f"core{g}", q)
        for i in range(*((0, 2), (2, 3))[g]):
            total = part[q, i, core] + crecv[q, i]
            xs[q, i] = total.astype(BF16).reshape(X, share, 1024)
            own = pl.ds(pl.multiple_of(x * share, share), share)
            xown[q, i] = part[q, i, core, own] + crecv[q, i, own]
        start(f"x{g}", q)

    def b2(q, g):
        arrived(f"x{g}", q)
        for i in range(*((0, 2), (2, 3))[g]):
            total = xown[q, i] + xr[q, 0, i].astype(F32) + xr[q, 1, i].astype(F32) + xr[q, 2, i].astype(F32)
            xown[q, i] = total
            xs[q, i, x] = total.astype(BF16)
        start(f"z{g}", q)

    def summed(q, i):
        return xown[q, i] + zr[q, i].astype(F32)

    def e_a(q):
        arrived("z0", q)
        gate, up = summed(q, 0), summed(q, 1)
        full[q, 0, core, x] = (gate * jax.nn.sigmoid(gate) * up).astype(BF16)
        start("back_x0", q)

    def e_b(q):
        arrived("z1", q)
        gate, up, grad = summed(q, 0), summed(q, 1), summed(q, 2)
        sigma = jax.nn.sigmoid(gate)
        full[q, 1, core, x] = (grad * up * sigma * (1.0 + gate * (1.0 - sigma))).astype(BF16)
        full[q, 2, core, x] = (grad * gate * sigma).astype(BF16)
        start("back_x1", q)

    def c1(q, g):
        arrived(f"back_x{g}", q)
        start(f"pass_x{g}", q)

    def c2(q, g):
        arrived(f"pass_x{g}", q)
        start(f"back_c{g}", q)

    def g2a(q):
        arrived("back_c0", q)
        block = full[q, 0].reshape(height, 1024)

        @pl.loop(0, 3)
        def _(n):
            cols = pl.ds(pl.multiple_of(n * 384, 384), 384)
            tmp[:, :, :, cols] = dot(block, dw[:, cols]).reshape(4, 2, rows, 384)

        ms[q] = tmp[...].astype(BF16)
        mown[q] = tmp[y]
        start("mix_y", q)
        hid_t[:, pl.ds(q * height, height)] = block.T
        out_copy(q, 2).start()

    def g2b(q):
        arrived("back_c1", q)
        out_copy(q, 3).start()
        out_copy(q, 4).start()
        left = full[q, 1].reshape(height, 1024)
        right = full[q, 2].reshape(height, 1024)

        @pl.loop(0, 3)
        def _(n):
            cols = pl.ds(pl.multiple_of(n * 384, 384), 384)
            tmp[:, :, :, cols] = (dot_t(left, gw[cols, :]) + dot_t(right, uw[cols, :])).reshape(4, 2, rows, 384)

        gs[q] = tmp[...].astype(BF16)
        gown[q] = tmp[:, zh]
        start("gt_z", q)

    def d1a(q):
        arrived("mix_y", q)
        mown[q] = mown[q] + mr[q, 0].astype(F32) + mr[q, 1].astype(F32) + mr[q, 2].astype(F32)
        mz[q] = mown[q, 1 - zh].astype(BF16)
        start("mix_z", q)

    def d1b(q):
        arrived("gt_z", q)
        total = gown[q] + gr[q].astype(F32)
        gown[q] = total
        gys[q] = total.astype(BF16)
        start("gt_y", q)

    def d2a(q):
        arrived("mix_z", q)
        mixed[mine(q), :] = (mown[q, zh] + mzr[q].astype(F32)).astype(BF16)

    def d2b(q):
        arrived("gt_y", q)
        grad_tokens[mine(q), :] = (
            gown[q, y] + gyr[q, 0].astype(F32) + gyr[q, 1].astype(F32) + gyr[q, 2].astype(F32)
        ).astype(BF16)

    stages = dict(
        a0=a0, a1t=a1t, a1c=a1c, g1a=g1a, g1b=g1b,
        b1a=lambda q: b1(q, 0), b1b=lambda q: b1(q, 1),
        b2a=lambda q: b2(q, 0), b2b=lambda q: b2(q, 1),
        ea=e_a, eb=e_b,
        c15a=lambda q: c1(q, 0), c15b=lambda q: c1(q, 1),
        c2a=lambda q: c2(q, 0), c2b=lambda q: c2(q, 1),
        g2a=g2a, g2b=g2b, d1a=d1a, d1b=d1b, d2a=d2a, d2b=d2b,
    )

    peers = [at_core, at_zl, at_zh] + [at_x(k) for k in (1, 2, 3)] + [at_y(k) for k in (1, 2, 3)]
    barrier = pltpu.get_barrier_semaphore()
    for peer in peers:
        pl.semaphore_signal(barrier, inc=1, device_id=peer, device_id_type=MESH)
    for q in range(CHUNKS):
        own_copy(q, 0).start()
        own_copy(q, 1).start()
    pl.semaphore_wait(barrier, len(peers))

    for step, (stage, q) in enumerate(PLAN):
        stages[stage](q)
        if step == 0:
            for i in range(3):
                load(i).start()

    @pl.loop(0, CHUNKS)
    def _(q):
        for name in COLUMNS:
            if not name.startswith("core"):
                sent(name, q)

    for q in range(CHUNKS):
        for i in range(5):
            out_copy(q, i).wait()


PLAN = (
    ("a0", 0), ("a0", 2), ("a1c", 0), ("a1t", 0), ("a1t", 2), ("a1c", 2), ("g1b", 0), ("g1a", 0),
    ("b1b", 0), ("b1a", 0), ("a0", 3), ("g1b", 2), ("b2b", 0), ("a0", 1), ("g1a", 2), ("a1t", 3),
    ("b1b", 2), ("b1a", 2), ("b2a", 0), ("a1c", 3), ("ea", 0), ("eb", 0), ("a1t", 1), ("g1a", 3),
    ("b2b", 2), ("b2a", 2), ("c15a", 0), ("b1a", 3), ("ea", 2), ("c15b", 0), ("c2a", 0), ("a1c", 1),
    ("g1b", 3), ("eb", 2), ("g1a", 1), ("b1b", 3), ("c2b", 0), ("b2a", 3), ("c15a", 2), ("g2a", 0),
    ("b1a", 1), ("c15b", 2), ("g2b", 0), ("g1b", 1), ("b2b", 3), ("c2a", 2), ("b1b", 1), ("ea", 3),
    ("g2a", 2), ("b2a", 1), ("eb", 3), ("c2b", 2), ("b2b", 1), ("c15a", 3), ("ea", 1), ("g2b", 2),
    ("c15b", 3), ("d1b", 0), ("d1a", 2), ("c2a", 3), ("eb", 1), ("g2a", 3), ("c15a", 1), ("c2b", 3),
    ("c15b", 1), ("g2b", 3), ("c2a", 1), ("d1b", 2), ("d2b", 0), ("c2b", 1), ("g2a", 1), ("g2b", 1),
    ("d2a", 2), ("d1b", 3), ("d1a", 0), ("d2b", 2), ("d1a", 3), ("d1b", 1), ("d1a", 1), ("d2a", 3),
    ("d2b", 3), ("d2a", 1), ("d2a", 0), ("d2b", 1),
)


def block(tokens, gate_weight, up_weight, down_weight, cotangent):
    n = CHUNKS
    rows, height = 128 // n, 1024 // n
    share = height // 8
    anyspace = pl.BlockSpec(memory_space=pl.ANY)
    vmem = pl.BlockSpec(memory_space=pltpu.VMEM)
    out_shape = [
        jax.ShapeDtypeStruct((128, 1152), BF16),
        jax.ShapeDtypeStruct((128, 1152), BF16),
        jax.ShapeDtypeStruct((1152, 1024), BF16),
        jax.ShapeDtypeStruct((n, Y, 2, rows, 1152), BF16),
        jax.ShapeDtypeStruct((1024, 1024), BF16),
        jax.ShapeDtypeStruct((n, 2, X, share, 1024), BF16),
        jax.ShapeDtypeStruct((n, 2, X, share, 1024), BF16),
    ]
    V = pltpu.VMEM
    scratch = [
        V((1152, 1024), BF16), V((1152, 1024), BF16), V((1024, 1152), BF16),
        V((n, Y, 2, rows, 1152), BF16), V((n, Y, 2, rows, 1152), BF16),
        V((n, 3, 2, height // 2, 1024), F32), V((n, 3, height // 2, 1024), F32),
        V((n, 3, X, share, 1024), BF16), V((n, 3, 3, share, 1024), BF16),
        V((n, 3, share, 1024), F32), V((n, 3, share, 1024), BF16),
        V((n, 3, 2, X, share, 1024), BF16),
        V((Y, 2, rows, 1152), F32), V((1152, 1024), BF16), V((1024, 1024), BF16),
        V((n, Y, 2, rows, 1152), BF16), V((n, 2, rows, 1152), F32), V((n, 3, 2, rows, 1152), BF16),
        V((n, rows, 1152), BF16), V((n, rows, 1152), BF16),
        V((n, Y, 2, rows, 1152), BF16), V((n, Y, rows, 1152), F32), V((n, Y, rows, 1152), BF16),
        V((n, Y, rows, 1152), BF16), V((n, 3, rows, 1152), BF16),
        pltpu.SemaphoreType.DMA((n, TOTAL)), pltpu.SemaphoreType.DMA((n, TOTAL)),
        pltpu.SemaphoreType.DMA((3,)), pltpu.SemaphoreType.DMA((n, 2)), pltpu.SemaphoreType.DMA((n, 5)),
    ]
    return pl.pallas_call(
        kernel,
        out_shape=out_shape,
        in_specs=[anyspace] * 5,
        out_specs=[vmem, vmem] + [anyspace] * 5,
        scratch_shapes=scratch,
        compiler_params=pltpu.CompilerParams(
            collective_id=0, has_side_effects=True, vmem_limit_bytes=63 << 20
        ),
        cost_estimate=pl.CostEstimate(flops=14_500_000_000, bytes_accessed=30_000_000, transcendentals=0),
        name="exchange",
    )(tokens, gate_weight, up_weight, down_weight, cotangent)


def gradients_kernel(
    tok, cot, hid, ggp, gup, mixed_in, tokens_in,
    grad_gate, grad_up, grad_down, mixed, grad_tokens,
    tok_v, cot_v, hid_v, ggp_v, gup_v, gate_v, up_v, down_v, small_v, in_sem, out_sem, pass_sem,
):
    pairs = ((tok, tok_v), (ggp, ggp_v), (gup, gup_v), (hid, hid_v), (cot, cot_v))
    loads = [pltpu.make_async_copy(src, dst, in_sem.at[i]) for i, (src, dst) in enumerate(pairs)]
    taken = [
        pltpu.make_async_copy(mixed_in, small_v.at[0], pass_sem.at[0]),
        pltpu.make_async_copy(tokens_in, small_v.at[1], pass_sem.at[1]),
    ]
    handed = [
        pltpu.make_async_copy(small_v.at[0], mixed, pass_sem.at[2]),
        pltpu.make_async_copy(small_v.at[1], grad_tokens, pass_sem.at[3]),
    ]
    loads[0].start()
    loads[1].start()

    def product(left, right, total, out, height, group):
        def write(n):
            part = pl.ds(pl.multiple_of(n * height, height), height)
            return pltpu.make_async_copy(total.at[part], out.at[part], out_sem.at[group, n])

        tiles = left.shape[0] // height

        @pl.loop(0, tiles)
        def _(n):
            part = pl.ds(pl.multiple_of(n * height, height), height)
            total[part, :] = dot(left[part, :], right[...])
            write(n).start()

        return [write(n) for n in range(tiles)]

    loads[0].wait()
    loads[1].wait()
    for copy in loads[2:] + taken:
        copy.start()
    writes = product(tok_v, ggp_v, gate_v, grad_gate, TILE_A, 0)
    for copy in taken:
        copy.wait()
    for copy in handed:
        copy.start()
    loads[2].wait()
    writes += product(tok_v, gup_v, up_v, grad_up, TILE_A, 1)
    loads[3].wait()
    loads[4].wait()
    writes += product(hid_v, cot_v, down_v, grad_down, TILE_B, 2)
    for copy in writes + handed:
        copy.wait()


TILE_A, TILE_B = 576, 512


def weight_gradients(rows_all, cot_all, hidden, ggp, gup, mixed, grad_tokens):
    wide, tall = (1024, 1152), (1152, 1024)
    square, small = (1024, 1024), (128, 1152)
    V = pltpu.VMEM
    anyspace = pl.BlockSpec(memory_space=pl.ANY)
    shapes = [jax.ShapeDtypeStruct(s, F32) for s in (tall, tall, wide)]
    return pl.pallas_call(
        gradients_kernel,
        out_shape=shapes + [jax.ShapeDtypeStruct(small, BF16)] * 2,
        in_specs=[anyspace] * 7,
        out_specs=[anyspace] * 5,
        scratch_shapes=[
            V(tall, BF16), V(wide, BF16), V(square, BF16), V(square, BF16), V(square, BF16),
            V(tall, F32), V(tall, F32), V(wide, F32), V((2,) + small, BF16),
            pltpu.SemaphoreType.DMA((5,)), pltpu.SemaphoreType.DMA((3, 8)), pltpu.SemaphoreType.DMA((4,)),
        ],
        compiler_params=pltpu.CompilerParams(vmem_limit_bytes=63 << 20),
        cost_estimate=pl.CostEstimate(flops=7_250_000_000, bytes_accessed=25_000_000, transcendentals=0),
        name="weight_gradients",
    )(rows_all, cot_all, hidden, ggp, gup, mixed, grad_tokens)


def on_device(tokens, gate_weight, up_weight, down_weight, cotangent):
    mixed, grad_tokens, rows_all, cot_all, hidden, ggp, gup = block(
        tokens, gate_weight, up_weight, down_weight, cotangent
    )
    cot_all = cot_all.reshape(1024, 1152)
    ggp, gup = ggp.reshape(1024, 1024), gup.reshape(1024, 1024)
    grad_gate, grad_up, grad_down, mixed, grad_tokens = weight_gradients(
        rows_all, cot_all, hidden, ggp, gup, mixed, grad_tokens
    )
    return (mixed, grad_tokens, grad_gate, grad_up, grad_down)


def solution(mesh):
    in_specs = (P("mp", "dp"), P("dp", "mp"), P("dp", "mp"), P("mp", "dp"), P("mp", "dp"))
    out_specs = (P("mp", "dp"), P("mp", "dp"), P("dp", "mp"), P("dp", "mp"), P("mp", "dp"))
    return jax.shard_map(
        on_device, mesh=mesh, in_specs=in_specs, out_specs=out_specs, check_vma=False
    )
```

```python
import functools

import jax
import jax.numpy as jnp
from jax import lax
from jax.experimental import pallas as pl
from jax.experimental.pallas import tpu as pltpu
from jax.sharding import PartitionSpec as P

MESH = pl.DeviceIdType.MESH
F32 = jnp.float32
BF16 = jnp.bfloat16
CHUNKS = 4
Y, X = 4, 4


def dot(left, right):
    return lax.dot_general(left, right, (((1,), (0,)), ((), ())), preferred_element_type=F32)


def dot_t(left, right):
    return lax.dot_general(left, right, (((1,), (1,)), ((), ())), preferred_element_type=F32)


def inner_rows(left, right):
    return lax.dot_general(left, right, (((0,), (0,)), ((), ())), preferred_element_type=F32)


COLUMNS = {}
for name, copies in (
    ("tok_z", 1), ("cot_y", 3), ("tok_y", 3), ("cot_z", 1),
    ("core0", 1), ("core1", 1), ("x0", 3), ("x1", 3), ("z0", 1), ("z1", 1),
    ("back_x0", 2), ("back_x1", 2), ("pass_x0", 2), ("pass_x1", 2), ("back_c0", 1), ("back_c1", 1),
    ("mix_y", 3), ("mix_z", 1), ("gt_z", 1), ("gt_y", 3),
):
    COLUMNS[name] = (sum(n for _, n in COLUMNS.values()), copies)
TOTAL = sum(n for _, n in COLUMNS.values())


def kernel(
    tokens, gate_w, up_w, down_w, cotangent,
    mixed, grad_tokens, tok_out, cot_out, hid_out, ggp_out, gup_out,
    gw, uw, dw, tok, cot, part, crecv, xs, xr, xown, zs, zr, full, tmp,
    ms, mown, mr, mz, mzr, gs, gown, gr, gys, gyr,
    send_sem, recv_sem, load_sem, own_sem, out_sem,
):
    rows = 128 // CHUNKS
    height = 1024 // CHUNKS
    share = height // 8
    dp, mp = lax.axis_index("dp"), lax.axis_index("mp")
    core = lax.rem(dp, 2)
    x = lax.rem(dp // 2, 4)
    zl = dp // 8
    y = mp // 2
    zh = lax.rem(mp, 2)

    def at_x(k):
        return (zl * 8 + lax.rem(x + k, 4) * 2 + core, mp)

    def at_y(k):
        return (dp, lax.rem(y + k, 4) * 2 + zh)

    at_core = (dp + 1 - 2 * core, mp)
    at_zl = (lax.rem(dp + 8, 16), mp)
    at_zh = (dp, mp + 1 - 2 * zh)

    def remote(name, q, j, src, dst, target):
        column = COLUMNS[name][0] + j
        return pltpu.make_async_remote_copy(
            src_ref=src, dst_ref=dst,
            send_sem=send_sem.at[q, column], recv_sem=recv_sem.at[q, column],
            device_id=target, device_id_type=MESH,
        )

    def mine(q):
        return pl.ds(pl.multiple_of(q * rows, rows), rows)

    def chunk_rows(q):
        return pl.ds(pl.multiple_of(q * height, height), height)

    GROUP = (slice(0, 2), slice(2, 3))
    BACK = (slice(0, 1), slice(1, 3))

    def copies(name, q):
        kind, g = name[:-1], None
        if name[-1] in "01":
            g = int(name[-1])
        if name == "tok_z":
            return [remote(name, q, 0, tokens.at[mine(q)], tok.at[q, y, zh], at_zh)]
        if name == "cot_y":
            return [remote(name, q, k - 1, cotangent.at[mine(q)], cot.at[q, y, zh], at_y(k)) for k in (2, 1, 3)]
        if name == "tok_y":
            return [remote(name, q, k - 1, tok.at[q, y], tok.at[q, y], at_y(k)) for k in (2, 1, 3)]
        if name == "cot_z":
            return [remote(name, q, 0, cot.at[q, :, zh], cot.at[q, :, zh], at_zh)]
        if kind == "core":
            return [remote(name, q, 0, part.at[q, GROUP[g], 1 - core], crecv.at[q, GROUP[g]], at_core)]
        if kind == "x":
            return [remote(name, q, k - 1, xs.at[q, GROUP[g], lax.rem(x + k, 4)], xr.at[q, k - 1, GROUP[g]], at_x(k)) for k in (2, 1, 3)]
        if kind == "z":
            return [remote(name, q, 0, zs.at[q, GROUP[g]], zr.at[q, GROUP[g]], at_zl)]
        if kind == "back_x":
            ref = full.at[q, BACK[g], core, x]
            return [remote(name, q, i, ref, ref, at_x(k)) for i, k in enumerate((1, 3))]
        if kind == "pass_x":
            result = []
            for i, k in enumerate((1, 3)):
                ref = full.at[q, BACK[g], core, lax.rem(x + 4 - k, 4), :, pl.ds(i * 512, 512)]
                result.append(remote(name, q, i, ref, ref, at_x(k)))
            return result
        if kind == "back_c":
            ref = full.at[q, BACK[g], core]
            return [remote(name, q, 0, ref, ref, at_core)]
        if name == "mix_y":
            return [remote(name, q, k - 1, ms.at[q, lax.rem(y + k, 4)], mr.at[q, k - 1], at_y(k)) for k in (2, 1, 3)]
        if name == "mix_z":
            return [remote(name, q, 0, mz.at[q], mzr.at[q], at_zh)]
        if name == "gt_z":
            return [remote(name, q, 0, gs.at[q, :, 1 - zh], gr.at[q], at_zh)]
        if name == "gt_y":
            return [remote(name, q, k - 1, gys.at[q, lax.rem(y + k, 4)], gyr.at[q, k - 1], at_y(k)) for k in (2, 1, 3)]

    def start(name, q):
        for copy in copies(name, q):
            copy.start()

    def arrived(name, q):
        for copy in copies(name, q):
            copy.wait_recv()

    def sent(name, q):
        for copy in copies(name, q):
            copy.wait_send()

    def own_copy(q, i):
        src, dst = ((tokens, tok), (cotangent, cot))[i]
        return pltpu.make_async_copy(src.at[mine(q)], dst.at[q, y, zh], own_sem.at[q, i])

    def load(i):
        src, dst = ((gate_w, gw), (up_w, uw), (down_w, dw))[i]
        return pltpu.make_async_copy(src, dst, load_sem.at[i])

    def out_copy(q, i):
        src = (tok.at[q], cot.at[q], full.at[q, 0], full.at[q, 1], full.at[q, 2])[i]
        dst = (tok_out, cot_out, hid_out, ggp_out, gup_out)[i].at[q]
        return pltpu.make_async_copy(src, dst, out_sem.at[q, i])

    def a0(q):
        start("tok_z", q)
        start("cot_y", q)

    def a1t(q):
        own_copy(q, 0).wait()
        arrived("tok_z", q)
        start("tok_y", q)

    def a1c(q):
        own_copy(q, 1).wait()
        arrived("cot_y", q)
        start("cot_z", q)

    def g1a(q):
        arrived("tok_y", q)
        if q == 0:
            load(0).wait()
            load(1).wait()
        out_copy(q, 0).start()
        block = tok[q].reshape(height, 1152)
        slot = q

        @pl.loop(0, 4)
        def _(n):
            cols = pl.ds(pl.multiple_of(n * 256, 256), 256)
            part[slot, 0, :, :, cols] = dot(block, gw[:, cols]).reshape(2, height // 2, 256)
            part[slot, 1, :, :, cols] = dot(block, uw[:, cols]).reshape(2, height // 2, 256)

        start("core0", q)

    def g1b(q):
        arrived("cot_z", q)
        if q == 0:
            load(2).wait()
        out_copy(q, 1).start()
        block = cot[q].reshape(height, 1152)
        slot = q

        @pl.loop(0, 4)
        def _(n):
            cols = pl.ds(pl.multiple_of(n * 256, 256), 256)
            part[slot, 2, :, :, cols] = dot_t(block, dw[cols, :]).reshape(2, height // 2, 256)

        start("core1", q)

    def b1(q, g):
        arrived(f"core{g}", q)
        sent(f"core{g}", q)
        for i in range(*((0, 2), (2, 3))[g]):
            total = part[q, i, core] + crecv[q, i]
            xs[q, i] = total.astype(BF16).reshape(X, share, 1024)
            own = pl.ds(pl.multiple_of(x * share, share), share)
            xown[q, i] = part[q, i, core, own] + crecv[q, i, own]
        start(f"x{g}", q)

    def b2(q, g):
        arrived(f"x{g}", q)
        for i in range(*((0, 2), (2, 3))[g]):
            total = xown[q, i] + xr[q, 0, i].astype(F32) + xr[q, 1, i].astype(F32) + xr[q, 2, i].astype(F32)
            xown[q, i] = total
            zs[q, i] = total.astype(BF16)
        start(f"z{g}", q)

    def summed(q, i):
        return xown[q, i] + zr[q, i].astype(F32)

    def e_a(q):
        arrived("z0", q)
        gate, up = summed(q, 0), summed(q, 1)
        full[q, 0, core, x] = (gate * jax.nn.sigmoid(gate) * up).astype(BF16)
        start("back_x0", q)

    def e_b(q):
        arrived("z1", q)
        gate, up, grad = summed(q, 0), summed(q, 1), summed(q, 2)
        sigma = jax.nn.sigmoid(gate)
        full[q, 1, core, x] = (grad * up * sigma * (1.0 + gate * (1.0 - sigma))).astype(BF16)
        full[q, 2, core, x] = (grad * gate * sigma).astype(BF16)
        start("back_x1", q)

    def c1(q, g):
        arrived(f"back_x{g}", q)
        start(f"pass_x{g}", q)

    def c2(q, g):
        arrived(f"pass_x{g}", q)
        start(f"back_c{g}", q)

    def g2a(q):
        arrived("back_c0", q)
        out_copy(q, 2).start()
        block = full[q, 0].reshape(height, 1024)

        @pl.loop(0, 3)
        def _(n):
            cols = pl.ds(pl.multiple_of(n * 384, 384), 384)
            tmp[:, :, :, cols] = dot(block, dw[:, cols]).reshape(4, 2, rows, 384)

        ms[q] = tmp[...].astype(BF16)
        mown[q] = tmp[y]
        start("mix_y", q)

    def g2b(q):
        arrived("back_c1", q)
        out_copy(q, 3).start()
        out_copy(q, 4).start()
        left = full[q, 1].reshape(height, 1024)
        right = full[q, 2].reshape(height, 1024)

        @pl.loop(0, 3)
        def _(n):
            cols = pl.ds(pl.multiple_of(n * 384, 384), 384)
            tmp[:, :, :, cols] = (dot_t(left, gw[cols, :]) + dot_t(right, uw[cols, :])).reshape(4, 2, rows, 384)

        gs[q] = tmp[...].astype(BF16)
        gown[q] = tmp[:, zh]
        start("gt_z", q)

    def d1a(q):
        arrived("mix_y", q)
        mown[q] = mown[q] + mr[q, 0].astype(F32) + mr[q, 1].astype(F32) + mr[q, 2].astype(F32)
        mz[q] = mown[q, 1 - zh].astype(BF16)
        start("mix_z", q)

    def d1b(q):
        arrived("gt_z", q)
        total = gown[q] + gr[q].astype(F32)
        gown[q] = total
        gys[q] = total.astype(BF16)
        start("gt_y", q)

    def d2a(q):
        arrived("mix_z", q)
        mixed[mine(q), :] = (mown[q, zh] + mzr[q].astype(F32)).astype(BF16)

    def d2b(q):
        arrived("gt_y", q)
        grad_tokens[mine(q), :] = (
            gown[q, y] + gyr[q, 0].astype(F32) + gyr[q, 1].astype(F32) + gyr[q, 2].astype(F32)
        ).astype(BF16)

    stages = dict(
        a0=a0, a1t=a1t, a1c=a1c, g1a=g1a, g1b=g1b,
        b1a=lambda q: b1(q, 0), b1b=lambda q: b1(q, 1),
        b2a=lambda q: b2(q, 0), b2b=lambda q: b2(q, 1),
        ea=e_a, eb=e_b,
        c15a=lambda q: c1(q, 0), c15b=lambda q: c1(q, 1),
        c2a=lambda q: c2(q, 0), c2b=lambda q: c2(q, 1),
        g2a=g2a, g2b=g2b, d1a=d1a, d1b=d1b, d2a=d2a, d2b=d2b,
    )

    peers = [at_core, at_zl, at_zh] + [at_x(k) for k in (1, 2, 3)] + [at_y(k) for k in (1, 2, 3)]
    barrier = pltpu.get_barrier_semaphore()
    for peer in peers:
        pl.semaphore_signal(barrier, inc=1, device_id=peer, device_id_type=MESH)
    for q in range(CHUNKS):
        own_copy(q, 0).start()
        own_copy(q, 1).start()
    pl.semaphore_wait(barrier, len(peers))

    for step, (stage, q) in enumerate(PLAN):
        stages[stage](q)
        if step == 0:
            for i in range(3):
                load(i).start()

    @pl.loop(0, CHUNKS)
    def _(q):
        for name in COLUMNS:
            if not name.startswith("core"):
                sent(name, q)
        for i in range(5):
            out_copy(q, i).wait()


PLAN = (
    ("a0", 0), ("a1t", 0), ("a0", 2), ("a1c", 0), ("a1t", 2), ("g1a", 0), ("a0", 1), ("a1c", 2),
    ("b1a", 0), ("g1b", 0), ("a0", 3), ("a1t", 1), ("b1b", 0), ("g1a", 2), ("g1b", 2), ("b2a", 0),
    ("b1a", 2), ("b2b", 0), ("ea", 0), ("a1c", 1), ("eb", 0), ("b1b", 2), ("g1a", 1), ("a1t", 3),
    ("a1c", 3), ("b1a", 1), ("b2a", 2), ("c15a", 0), ("g1b", 1), ("b2b", 2), ("c15b", 0), ("b1b", 1),
    ("b2a", 1), ("g1a", 3), ("c2b", 0), ("ea", 2), ("c2a", 0), ("eb", 2), ("ea", 1), ("g2b", 0),
    ("g1b", 3), ("c15a", 2), ("b1a", 3), ("c15b", 2), ("b1b", 3), ("g2a", 0), ("b2b", 1), ("c2a", 2),
    ("g2a", 2), ("eb", 1), ("b2a", 3), ("c15a", 1), ("d1b", 0), ("c2b", 2), ("d1a", 0), ("ea", 3),
    ("b2b", 3), ("g2b", 2), ("c15b", 1), ("c2a", 1), ("eb", 3), ("g2a", 1), ("c15a", 3), ("c2b", 1),
    ("d1a", 2), ("c15b", 3), ("g2b", 1), ("d1b", 2), ("d2a", 0), ("c2a", 3), ("c2b", 3), ("g2a", 3),
    ("g2b", 3), ("d2b", 0), ("d1b", 1), ("d1a", 3), ("d1a", 1), ("d1b", 3), ("d2a", 2), ("d2b", 2),
    ("d2a", 1), ("d2a", 3), ("d2b", 1), ("d2b", 3),
)


def block(tokens, gate_weight, up_weight, down_weight, cotangent):
    n = CHUNKS
    rows, height = 128 // n, 1024 // n
    share = height // 8
    anyspace = pl.BlockSpec(memory_space=pl.ANY)
    vmem = pl.BlockSpec(memory_space=pltpu.VMEM)
    out_shape = [
        jax.ShapeDtypeStruct((128, 1152), BF16),
        jax.ShapeDtypeStruct((128, 1152), BF16),
        jax.ShapeDtypeStruct((n, Y, 2, rows, 1152), BF16),
        jax.ShapeDtypeStruct((n, Y, 2, rows, 1152), BF16),
        jax.ShapeDtypeStruct((n, 2, X, share, 1024), BF16),
        jax.ShapeDtypeStruct((n, 2, X, share, 1024), BF16),
        jax.ShapeDtypeStruct((n, 2, X, share, 1024), BF16),
    ]
    V = pltpu.VMEM
    scratch = [
        V((1152, 1024), BF16), V((1152, 1024), BF16), V((1024, 1152), BF16),
        V((n, Y, 2, rows, 1152), BF16), V((n, Y, 2, rows, 1152), BF16),
        V((n, 3, 2, height // 2, 1024), F32), V((n, 3, height // 2, 1024), F32),
        V((n, 3, X, share, 1024), BF16), V((n, 3, 3, share, 1024), BF16),
        V((n, 3, share, 1024), F32), V((n, 3, share, 1024), BF16), V((n, 3, share, 1024), BF16),
        V((n, 3, 2, X, share, 1024), BF16),
        V((Y, 2, rows, 1152), F32),
        V((n, Y, 2, rows, 1152), BF16), V((n, 2, rows, 1152), F32), V((n, 3, 2, rows, 1152), BF16),
        V((n, rows, 1152), BF16), V((n, rows, 1152), BF16),
        V((n, Y, 2, rows, 1152), BF16), V((n, Y, rows, 1152), F32), V((n, Y, rows, 1152), BF16),
        V((n, Y, rows, 1152), BF16), V((n, 3, rows, 1152), BF16),
        pltpu.SemaphoreType.DMA((n, TOTAL)), pltpu.SemaphoreType.DMA((n, TOTAL)),
        pltpu.SemaphoreType.DMA((3,)), pltpu.SemaphoreType.DMA((n, 2)), pltpu.SemaphoreType.DMA((n, 5)),
    ]
    return pl.pallas_call(
        kernel,
        out_shape=out_shape,
        in_specs=[anyspace] * 5,
        out_specs=[vmem, vmem] + [anyspace] * 5,
        scratch_shapes=scratch,
        compiler_params=pltpu.CompilerParams(
            collective_id=0, has_side_effects=True, vmem_limit_bytes=63 << 20
        ),
        cost_estimate=pl.CostEstimate(flops=14_500_000_000, bytes_accessed=30_000_000, transcendentals=0),
        name="exchange",
    )(tokens, gate_weight, up_weight, down_weight, cotangent)


def gradients_kernel(
    tok, cot, hid, ggp, gup, grad_gate, grad_up, grad_down,
    tok_v, cot_v, hid_v, ggp_v, gup_v, gate_v, up_v, down_v, in_sem, out_sem,
):
    pairs = ((tok, tok_v), (ggp, ggp_v), (gup, gup_v), (hid, hid_v), (cot, cot_v))
    loads = [pltpu.make_async_copy(src, dst, in_sem.at[i]) for i, (src, dst) in enumerate(pairs)]
    loads[0].start()
    loads[1].start()

    def product(left, right, total, out, height, group):
        def write(m):
            part = pl.ds(pl.multiple_of(m * height, height), height)
            return pltpu.make_async_copy(total.at[part], out.at[part], out_sem.at[group, m])

        tiles = left.shape[1] // height

        @pl.loop(0, tiles)
        def _(m):
            part = pl.ds(pl.multiple_of(m * height, height), height)
            total[part, :] = inner_rows(left[:, part], right[...])
            write(m).start()

        return [write(m) for m in range(tiles)]

    loads[0].wait()
    loads[1].wait()
    for copy in loads[2:]:
        copy.start()
    writes = product(tok_v, ggp_v, gate_v, grad_gate, TILE_A, 0)
    loads[2].wait()
    writes += product(tok_v, gup_v, up_v, grad_up, TILE_A, 1)
    loads[3].wait()
    loads[4].wait()
    writes += product(hid_v, cot_v, down_v, grad_down, TILE_B, 2)
    for copy in writes:
        copy.wait()


TILE_A, TILE_B = 384, 256


def weight_gradients(rows_all, cot_all, hidden, ggp, gup):
    wide, tall = (1024, 1152), (1152, 1024)
    square = (1024, 1024)
    V = pltpu.VMEM
    anyspace = pl.BlockSpec(memory_space=pl.ANY)
    return pl.pallas_call(
        gradients_kernel,
        out_shape=[jax.ShapeDtypeStruct(s, F32) for s in (tall, tall, wide)],
        in_specs=[anyspace] * 5,
        out_specs=[anyspace] * 3,
        scratch_shapes=[
            V(wide, BF16), V(wide, BF16), V(square, BF16), V(square, BF16), V(square, BF16),
            V(tall, F32), V(tall, F32), V(wide, F32),
            pltpu.SemaphoreType.DMA((5,)), pltpu.SemaphoreType.DMA((3, 8)),
        ],
        compiler_params=pltpu.CompilerParams(vmem_limit_bytes=63 << 20),
        cost_estimate=pl.CostEstimate(flops=7_250_000_000, bytes_accessed=25_000_000, transcendentals=0),
        name="weight_gradients",
    )(rows_all, cot_all, hidden, ggp, gup)


def on_device(tokens, gate_weight, up_weight, down_weight, cotangent):
    mixed, grad_tokens, rows_all, cot_all, hidden, ggp, gup = block(
        tokens, gate_weight, up_weight, down_weight, cotangent
    )
    rows_all = rows_all.reshape(1024, 1152)
    cot_all = cot_all.reshape(1024, 1152)
    hidden, ggp, gup = (a.reshape(1024, 1024) for a in (hidden, ggp, gup))
    grad_gate, grad_up, grad_down = weight_gradients(rows_all, cot_all, hidden, ggp, gup)
    return (mixed, grad_tokens, grad_gate, grad_up, grad_down)


def solution(mesh):
    in_specs = (P("mp", "dp"), P("dp", "mp"), P("dp", "mp"), P("mp", "dp"), P("mp", "dp"))
    out_specs = (P("mp", "dp"), P("mp", "dp"), P("dp", "mp"), P("dp", "mp"), P("mp", "dp"))
    return jax.shard_map(
        on_device, mesh=mesh, in_specs=in_specs, out_specs=out_specs, check_vma=False
    )
```
